32 devices in a mesh: groups: 2 (over y), tok: 4 (over x, core), blk: 4 (over z).
Axes of the slice: x: 2, y: 2, z: 4, core: 2. Of those that a mesh axis runs over, the one named last changes fastest.
Arguments:
- activations: bfloat16 [2048, 6144], P(('groups', 'tok')), parts along dimension 0, may hold values from -6 to 6
- directions: float32 [12288, 256], P(('groups', 'tok'), 'blk'), parts along dimension 0, may hold values from -6 to 6
- block_rank: int32 [4], replicated, may hold values from 0 to 3, each once
Outputs:
- updated: float32 [12288, 256], P(('groups', 'tok'), 'blk'), parts along dimension 0
The draws below stay inside these ranges and needn't reach their ends.
There are 2 independent parts, one for each index of `groups`. The reference program is written for one: setup_inputs(seed, part) draws one part's arguments, and reference() takes and returns one part's arrays. A program takes and returns all parts, laid end to end along the dimension named above; an argument that names none is the same for every part. Nothing has to cross between parts.
Inputs may be any that keep to these rules, and one draw needn't show every extreme that they name: `block_rank`: a permutation of the block numbers.
All inputs are finite; a program needn't handle non-finite values.
Results may differ from the reference program's by a relative error of at most 0.006.
Values may be sent and summed in bfloat16 or wider, within the bound.
A program may use at most 64 MiB of HBM per device.

```python
import jax
import jax.numpy as jnp
from jax import lax

D = 6144
BW = 64
ITERS = 3
NB = 4
K = 256
TOKENS = 1024


def with_spikes(drawn, key, source, target, shards_of, factor):
    def block_of(axis_at):
        return (jnp.arange(drawn.shape[axis_at]) // (drawn.shape[axis_at] // shards_of)).reshape((-1,) + (1,) * (drawn.ndim - 1 - axis_at))

    near = jax.random.permutation(key, shards_of)[block_of(target)]
    other_side = (block_of(target) + shards_of // 2) % shards_of
    return jnp.where((block_of(source) == near) | (block_of(source) == other_side), factor * drawn, drawn)


def levels(stream_key, shape, split, smallest, top_value):
    def one(dim, parts):
        heights = jax.random.uniform(jax.random.fold_in(jax.random.fold_in(stream_key, 6), dim), (parts,), jnp.float32, smallest / len(split), top_value / len(split))
        return jnp.repeat(jnp.exp(heights), shape[dim] // parts).reshape((-1,) + (1,) * (len(shape) - dim - 1))

    loudness = one(*split[0])
    for cut in split[1:]:
        loudness = loudness * one(*cut)
    return loudness


def noise(stream_key, shape, scale, limit, pieces=(), kind=jnp.bfloat16):
    drawn = scale * jax.random.normal(stream_key, shape, jnp.float32)
    if pieces:
        drawn = drawn * levels(stream_key, shape, pieces, -0.22, 0.18)
    return jnp.clip(drawn, -limit, limit).astype(kind)


def noise_with(own_key, extent, scale, limit, pieces, heavy, kind=jnp.bfloat16):
    values = scale * jax.random.normal(own_key, extent, jnp.float32)
    if pieces:
        values = values * levels(own_key, extent, pieces, -0.22, 0.18)
    return jnp.clip(with_spikes(values, jax.random.fold_in(own_key, 3), *heavy), -limit, limit).astype(kind)


def setup_inputs(seed: int = 0, part: int = 0) -> dict:
    streams_of = jax.random.split(jax.random.key(seed), 4)
    part_splits = jax.random.split(jax.random.fold_in(streams_of[3], part), 4)
    activations = noise_with(part_splits[0], (TOKENS, D), 1.0, 6.0, ((0, 4),), (0, 1, 4, 2.0))
    directions = noise(part_splits[1], (D, K), 1.0, 6.0, ((0, 4), (1, 4)), jnp.float32)
    block_rank = jax.random.permutation(streams_of[2], NB).astype(jnp.int32)
    return {"activations": activations, "directions": directions, "block_rank": block_rank}


def order_mask(block_rank, count):
    index = jnp.arange(count, dtype=jnp.int32)
    blocks = index // BW
    table = (blocks[:, None] == jnp.arange(NB, dtype=jnp.int32)[None, :]).astype(jnp.int32)
    ranks = lax.optimization_barrier(jnp.sum(table * block_rank[None, :], axis=1))
    before = ranks[None, :] < ranks[:, None]
    inside = (blocks[None, :] == blocks[:, None]) & (index[None, :] < index[:, None])
    return (before | inside).astype(jnp.float32)

def split_parts(weighted):
    high = lax.optimization_barrier(weighted.astype(jnp.bfloat16))
    rest = (weighted - high.astype(jnp.float32)).astype(jnp.bfloat16)
    return (high, rest)

def reference(activations, directions, block_rank):
    mask = order_mask(block_rank, K)
    current = directions
    for step in range(ITERS):
        low = current.astype(jnp.bfloat16)
        proj = jnp.dot(activations, low, preferred_element_type=jnp.float32).astype(jnp.bfloat16)
        cov_dir = lax.dot_general(activations, proj, (((0,), (0,)), ((), ())), preferred_element_type=jnp.float32) / TOKENS
        cross = lax.dot_general(proj, proj, (((0,), (0,)), ((), ())), preferred_element_type=jnp.float32) / (TOKENS * D)
        high, rest = split_parts(mask * cross)
        contract = (((1,), (1,)), ((), ()))
        penalty = lax.dot_general(low, high, contract, preferred_element_type=jnp.float32) + lax.dot_general(low, rest, contract, preferred_element_type=jnp.float32)
        moved = current + 0.5 * (cov_dir - penalty)
        scale = jnp.sqrt(lax.optimization_barrier(jnp.mean(moved * moved, axis=0)) + 1e-06)
        current = moved / scale[None, :]
    return current
```

```python
import functools

import jax
import jax.numpy as jnp
from jax import lax
from jax.experimental import pallas as pl
from jax.experimental.pallas import tpu as pltpu
from jax.sharding import PartitionSpec as P

BW = 64
ITERS = 3


def block_ranks(block_rank, index):
    blocks = index // BW
    table = (blocks[:, None] == jnp.arange(block_rank.shape[0], dtype=jnp.int32)[None, :]).astype(
        jnp.int32
    )
    return (blocks, jnp.sum(table * block_rank[None, :], axis=1))


def split_parts(weighted):
    high = lax.optimization_barrier(weighted.astype(jnp.bfloat16))
    rest = (weighted - high.astype(jnp.float32)).astype(jnp.bfloat16)
    return (high, rest)


def body(activations, directions, block_rank):
    width = activations.shape[1]
    total_tokens = activations.shape[0] * lax.axis_size("tok")
    count = BW * lax.axis_size("blk")
    mine = lax.axis_index("blk")
    own_index = mine * BW + jnp.arange(BW, dtype=jnp.int32)
    all_index = jnp.arange(count, dtype=jnp.int32)
    own_blocks, own_ranks = block_ranks(block_rank, own_index)
    all_blocks, all_ranks = block_ranks(block_rank, all_index)
    contract = (((1,), (1,)), ((), ()))
    features = lax.all_to_all(activations, "tok", split_axis=1, concat_axis=0, tiled=True)
    current = directions
    for step in range(ITERS):
        low = current.astype(jnp.bfloat16)
        proj = jnp.dot(
            activations,
            lax.all_gather(low, "tok", axis=0, tiled=True),
            preferred_element_type=jnp.float32,
        ).astype(jnp.bfloat16)
        cov_dir = (
            lax.dot_general(
                features,
                lax.all_gather(proj, "tok", axis=0, tiled=True),
                (((0,), (0,)), ((), ())),
                preferred_element_type=jnp.float32,
            )
            / total_tokens
        )
        partial_rows = lax.dot_general(
            proj,
            lax.all_gather(proj, "blk", axis=1, tiled=True),
            (((0,), (0,)), ((), ())),
            preferred_element_type=jnp.float32,
        )
        cross_row = lax.psum(partial_rows, "tok") / (total_tokens * width)
        before = all_ranks[None, :] < own_ranks[:, None]
        inside = (all_blocks[None, :] == own_blocks[:, None]) & (
            all_index[None, :] < own_index[:, None]
        )
        high, rest = split_parts((before | inside).astype(jnp.float32) * cross_row)
        piece = lax.all_gather(low, "blk", axis=1, tiled=True)
        total = lax.dot_general(piece, high, contract, preferred_element_type=jnp.float32)
        penalty = total + lax.dot_general(piece, rest, contract, preferred_element_type=jnp.float32)
        moved = current + 0.5 * (cov_dir - penalty)
        squares = lax.psum(jnp.sum(moved * moved, axis=0), "tok")
        scale = jnp.sqrt(squares / width + 1e-06)
        current = moved / scale[None, :]
    return current


F32, BF16 = jnp.float32, jnp.bfloat16
MESH = pl.DeviceIdType.MESH


def nt(a, b):
    return lax.dot_general(a, b, (((1,), (1,)), ((), ())), preferred_element_type=F32)


def nn(a, b):
    return jnp.dot(a, b, preferred_element_type=F32)


def order_mask(rank_ref, m, count):
    rows = lax.broadcasted_iota(jnp.int32, (count, count), 0)
    cols = lax.broadcasted_iota(jnp.int32, (count, count), 1)
    row_rank = jnp.zeros((count, count), jnp.int32)
    col_rank = jnp.zeros((count, count), jnp.int32)
    same = jnp.zeros((count, count), jnp.int32)
    for k in range(m):
        in_row = (rows >= k * BW) & (rows < (k + 1) * BW)
        in_col = (cols >= k * BW) & (cols < (k + 1) * BW)
        row_rank = jnp.where(in_row, rank_ref[k], row_rank)
        col_rank = jnp.where(in_col, rank_ref[k], col_rank)
        same = jnp.where(in_row & in_col, 1, same)
    inside = (same == 1) & (cols < rows)
    return jnp.where((col_rank < row_rank) | inside, 1.0, 0.0).astype(F32)


def fused(
    n, m, rank_ref, act_ref, dir_ref, out_ref,
    feat, low, v32, u32, chain, part, arrived, proj, wsum, half, coef, sq_out, sq_in,
    f_loc, f_s, f_r, v_s, v_r, p_s, p_r, k_s, k_r, q_s, q_r,
):
    i, b = lax.axis_index("tok"), lax.axis_index("blk")
    tokens, rows = feat.shape[1], feat.shape[2]
    count = m * BW
    total_tokens, width = n * tokens, n * rows
    own = pl.ds(pl.multiple_of(b * BW, BW), BW)

    def ahead(d):
        return lax.rem(i + d, n)

    def behind(d):
        return lax.rem(i + n - d, n)

    def blk_ahead(d):
        return lax.rem(b + d, m)

    def blk_behind(d):
        return lax.rem(b + m - d, m)

    others = [(d, e) for e in range(m) for d in range(n) if (d, e) != (0, 0)]

    barrier = pltpu.get_barrier_semaphore()
    for d, e in others:
        pl.semaphore_signal(
            barrier, inc=1, device_id={"tok": ahead(d), "blk": blk_ahead(e)}, device_id_type=MESH
        )
    pl.semaphore_wait(barrier, len(others))

    sent = []

    def push(src, dst, s, r, d, e):
        copy = pltpu.make_async_remote_copy(
            src_ref=src, dst_ref=dst, send_sem=s, recv_sem=r,
            device_id={"tok": ahead(d), "blk": blk_ahead(e)}, device_id_type=MESH,
        )
        copy.start()
        sent.append(copy)

    def landed(dst, s, r):
        pltpu.make_async_remote_copy(
            src_ref=dst, dst_ref=dst, send_sem=s, recv_sem=r,
            device_id={"tok": ahead(1)}, device_id_type=MESH,
        ).wait_recv()

    for d in range(1, n):
        cols = pl.ds(pl.multiple_of(ahead(d) * rows, 128), rows)
        push(act_ref.at[:, cols], feat.at[i], f_s.at[d], f_r.at[d], d, 0)
    mine = pltpu.make_async_copy(
        act_ref.at[:, pl.ds(pl.multiple_of(i * rows, 128), rows)], feat.at[i], f_loc
    )
    mine.start()
    v32[...] = dir_ref[...].T
    low[own, :] = v32[...].astype(BF16)
    for e in range(1, m):
        push(low.at[own], low.at[own], v_s.at[e], v_r.at[e], 0, e)
    mask = order_mask(rank_ref, m, count)
    mine.wait()

    def scatter(k, left, first):
        kept = nt(left, feat[i])
        for d in range(1, n):
            j = ahead(d)
            if first:
                landed(feat.at[behind(n - d)], f_s.at[n - d], f_r.at[n - d])
            part[k, d] = nt(left, feat[j])
            push(part.at[k, d], arrived.at[k, d], p_s.at[k, d], p_r.at[k, d], d, 0)
        return kept

    def gather(k, kept):
        for d in range(1, n):
            landed(arrived.at[k, d], p_s.at[k, d], p_r.at[k, d])
            kept = kept + arrived[k, d]
        chain[k, i, own, :] = kept.astype(BF16)
        for d, e in others:
            tile = chain.at[k, i, own]
            push(tile, tile, k_s.at[k, d, e], k_r.at[k, d, e], d, e)

    def chain_landed(k, d, e):
        peer = pl.ds(pl.multiple_of(blk_behind(e) * BW, BW), BW)
        landed(chain.at[k, behind(d), peer], k_s.at[k, d, e], k_r.at[k, d, e])

    def to_features(k):
        total = nn(chain[k, i, own, :], feat[i])
        for d in range(1, n):
            chain_landed(k, d, 0)
            j = behind(d)
            total = total + nn(chain[k, j, own, :], feat[j])
        return total * (0.5 / total_tokens)

    def rest_landed(k):
        for e in range(1, m):
            for d in range(n):
                chain_landed(k, d, e)

    def penalised(t, cross):
        half[t] = mask * cross * (0.5 / (total_tokens * width))

    def send_squares(t, moved, everyone):
        column = jnp.sum(moved * moved, axis=1, keepdims=True)
        block = jnp.concatenate(
            [jnp.broadcast_to(column, (BW, 128)), jnp.zeros((128 - BW, 128), F32)], axis=0
        )
        sq_in[t, 0, 0] = block.T[0:8]
        for d, e in others:
            if everyone or e == 0:
                push(sq_in.at[t, 0, 0], sq_in.at[t, d, e], q_s.at[t, d, e], q_r.at[t, d, e], d, e)

    def scale_of(t, e):
        total = sq_in[t, 0, e]
        for d in range(1, n):
            total = total + sq_in[t, d, e]
        column = jnp.broadcast_to(total[0:1], (128, 128)).T[0:BW]
        return lax.rsqrt(column * (1.0 / width) + 1e-06)

    def scales(t):
        for d, e in others:
            landed(sq_in.at[t, d, e], q_s.at[t, d, e], q_r.at[t, d, e])
        for e in range(m):
            where = pl.ds(pl.multiple_of(blk_behind(e) * BW, BW), BW)
            sq_out[where, :] = scale_of(t, e)
        return sq_out[:, 0:1]

    def combine(c_rows, weights):
        lane = lax.broadcasted_iota(jnp.int32, (BW, count), 1)
        line = lax.broadcasted_iota(jnp.int32, (BW, count), 0) + b * BW
        diag = jnp.sum(jnp.where(lane == line, c_rows, 0.0), axis=1, keepdims=True)
        off = jnp.where(lane == line, 0.0, c_rows)
        moved = diag * v32[...] + nn(off.astype(BF16), low[...])
        for j in range(n):
            moved = moved + nn(weights(j).astype(BF16), feat[j])
        return moved

    kept = scatter(0, low[own, :], True)
    gather(0, kept)
    u32[...] = to_features(0)
    kept = scatter(1, u32[...].astype(BF16), False)
    gather(1, kept)
    second = to_features(1).astype(BF16)
    kept = scatter(2, second, False)

    rest_landed(0)
    for e in range(1, m):
        peer = pl.ds(pl.multiple_of(blk_behind(e) * BW, BW), BW)
        landed(low.at[peer], v_s.at[e], v_r.at[e])
    cross = jnp.zeros((count, count), F32)
    for j in range(n):
        cross = cross + nt(chain[0, j], chain[0, j])
    penalised(0, cross)
    moved = v32[...] + u32[...] - nn(half[0, own, :].astype(BF16), low[...])
    send_squares(0, moved, True)
    gather(2, kept)

    rest_landed(1)
    d0 = scales(0)
    h0 = half[0].astype(BF16)
    cross = jnp.zeros((count, count), F32)
    for j in range(n):
        k0 = chain[0, j]
        p1 = d0 * (k0.astype(F32) - nn(h0, k0) + chain[1, j].astype(F32))
        proj[j] = p1
        cross = cross + nt(p1.astype(BF16), p1.astype(BF16))
    penalised(1, cross)
    h1 = half[1].astype(BF16)
    eye = jnp.where(
        lax.broadcasted_iota(jnp.int32, (count, count), 0)
        == lax.broadcasted_iota(jnp.int32, (count, count), 1), 1.0, 0.0,
    )
    c1 = d0 * (eye - half[0])
    coef[...] = c1 - nn(h1, c1.astype(BF16))
    for j in range(n):
        w1 = d0 * chain[0, j].astype(F32) * (0.5 / total_tokens)
        wsum[j] = w1 - nn(h1, w1.astype(BF16)) + proj[j] * (0.5 / total_tokens)
    moved = combine(coef[own, :], lambda j: wsum[j, own, :])
    send_squares(1, moved, True)

    for d in range(1, n):
        chain_landed(2, d, 0)
    rest_landed(2)
    for j in range(n):
        k1 = chain[1, j]
        q1 = d0 * (k1.astype(F32) - nn(h0, k1) + chain[2, j].astype(F32))
        p1 = proj[j]
        proj[j] = p1 - nn(h1, p1.astype(BF16)) + q1
    d1 = scales(1)
    cross = jnp.zeros((count, count), F32)
    for j in range(n):
        p2 = d1 * proj[j]
        proj[j] = p2
        wsum[j] = d1 * wsum[j]
        cross = cross + nt(p2.astype(BF16), p2.astype(BF16))
    penalised(2, cross)
    coef[...] = d1 * coef[...]
    h2 = half[2, own, :].astype(BF16)
    c3 = coef[own, :] - nn(h2, coef[...].astype(BF16))

    def last_weights(j):
        return (
            wsum[j, own, :] - nn(h2, wsum[j].astype(BF16)) + proj[j, own, :] * (0.5 / total_tokens)
        )

    moved = combine(c3, last_weights)
    send_squares(2, moved, False)
    v32[...] = moved
    for d in range(1, n):
        landed(sq_in.at[2, d, 0], q_s.at[2, d, 0], q_r.at[2, d, 0])
    out_ref[...] = (v32[...] * scale_of(2, 0)[:, 0:1]).T
    for copy in sent:
        copy.wait_send()


def fused_body(n, m, activations, directions, block_rank):
    tokens = activations.shape[0]
    rows = directions.shape[0]
    count = m * BW
    dma = pltpu.SemaphoreType.DMA
    return pl.pallas_call(
        functools.partial(fused, n, m),
        out_shape=jax.ShapeDtypeStruct((rows, BW), F32),
        in_specs=[
            pl.BlockSpec(memory_space=pltpu.SMEM),
            pl.BlockSpec(memory_space=pl.ANY),
            pl.BlockSpec(memory_space=pltpu.VMEM),
        ],
        out_specs=pl.BlockSpec(memory_space=pltpu.VMEM),
        scratch_shapes=[
            pltpu.VMEM((n, tokens, rows), BF16),
            pltpu.VMEM((count, rows), BF16),
            pltpu.VMEM((BW, rows), F32),
            pltpu.VMEM((BW, rows), F32),
            pltpu.VMEM((ITERS, n, count, tokens), BF16),
            pltpu.VMEM((ITERS, n, BW, tokens), F32),
            pltpu.VMEM((ITERS, n, BW, tokens), F32),
            pltpu.VMEM((n, count, tokens), F32),
            pltpu.VMEM((n, count, tokens), F32),
            pltpu.VMEM((ITERS, count, count), F32),
            pltpu.VMEM((count, count), F32),
            pltpu.VMEM((count, 128), F32),
            pltpu.VMEM((ITERS, n, m, 8, 128), F32),
            dma,
            dma((n,)), dma((n,)),
            dma((m,)), dma((m,)),
            dma((ITERS, n)), dma((ITERS, n)),
            dma((ITERS, n, m)), dma((ITERS, n, m)),
            dma((ITERS, n, m)), dma((ITERS, n, m)),
        ],
        compiler_params=pltpu.CompilerParams(
            collective_id=0, has_side_effects=True, vmem_limit_bytes=48 * 1024 * 1024
        ),
    )(block_rank, activations, directions)


def solution(mesh):
    n, m = mesh.shape["tok"], mesh.shape["blk"]
    placed = (P(("groups", "tok"), None), P(("groups", "tok"), "blk"), P())

    def chosen(activations, directions, block_rank):
        held = n * m * BW * activations.shape[0] * (3 * 2 + 2 * 4)
        if held <= 16 * 1024 * 1024:
            return fused_body(n, m, activations, directions, block_rank)
        return body(activations, directions, block_rank)

    return jax.shard_map(
        chosen, mesh=mesh, in_specs=placed, out_specs=P(("groups", "tok"), "blk"), check_vma=False
    )
```

```python
import functools

import jax
import jax.numpy as jnp
from jax import lax
from jax.experimental import pallas as pl
from jax.experimental.pallas import tpu as pltpu
from jax.sharding import PartitionSpec as P

BW = 64
ITERS = 3


def block_ranks(block_rank, index):
    blocks = index // BW
    table = (blocks[:, None] == jnp.arange(block_rank.shape[0], dtype=jnp.int32)[None, :]).astype(
        jnp.int32
    )
    return (blocks, jnp.sum(table * block_rank[None, :], axis=1))


def split_parts(weighted):
    high = lax.optimization_barrier(weighted.astype(jnp.bfloat16))
    rest = (weighted - high.astype(jnp.float32)).astype(jnp.bfloat16)
    return (high, rest)


def body(activations, directions, block_rank):
    width = activations.shape[1]
    total_tokens = activations.shape[0] * lax.axis_size("tok")
    count = BW * lax.axis_size("blk")
    mine = lax.axis_index("blk")
    own_index = mine * BW + jnp.arange(BW, dtype=jnp.int32)
    all_index = jnp.arange(count, dtype=jnp.int32)
    own_blocks, own_ranks = block_ranks(block_rank, own_index)
    all_blocks, all_ranks = block_ranks(block_rank, all_index)
    contract = (((1,), (1,)), ((), ()))
    features = lax.all_to_all(activations, "tok", split_axis=1, concat_axis=0, tiled=True)
    current = directions
    for step in range(ITERS):
        low = current.astype(jnp.bfloat16)
        proj = jnp.dot(
            activations,
            lax.all_gather(low, "tok", axis=0, tiled=True),
            preferred_element_type=jnp.float32,
        ).astype(jnp.bfloat16)
        cov_dir = (
            lax.dot_general(
                features,
                lax.all_gather(proj, "tok", axis=0, tiled=True),
                (((0,), (0,)), ((), ())),
                preferred_element_type=jnp.float32,
            )
            / total_tokens
        )
        partial_rows = lax.dot_general(
            proj,
            lax.all_gather(proj, "blk", axis=1, tiled=True),
            (((0,), (0,)), ((), ())),
            preferred_element_type=jnp.float32,
        )
        cross_row = lax.psum(partial_rows, "tok") / (total_tokens * width)
        before = all_ranks[None, :] < own_ranks[:, None]
        inside = (all_blocks[None, :] == own_blocks[:, None]) & (
            all_index[None, :] < own_index[:, None]
        )
        high, rest = split_parts((before | inside).astype(jnp.float32) * cross_row)
        piece = lax.all_gather(low, "blk", axis=1, tiled=True)
        total = lax.dot_general(piece, high, contract, preferred_element_type=jnp.float32)
        penalty = total + lax.dot_general(piece, rest, contract, preferred_element_type=jnp.float32)
        moved = current + 0.5 * (cov_dir - penalty)
        squares = lax.psum(jnp.sum(moved * moved, axis=0), "tok")
        scale = jnp.sqrt(squares / width + 1e-06)
        current = moved / scale[None, :]
    return current


F32, BF16 = jnp.float32, jnp.bfloat16
MESH = pl.DeviceIdType.MESH


def nt(a, b):
    return lax.dot_general(a, b, (((1,), (1,)), ((), ())), preferred_element_type=F32)


def nn(a, b):
    return jnp.dot(a, b, preferred_element_type=F32)


def order_mask(rank_ref, m, count):
    rows = lax.broadcasted_iota(jnp.int32, (count, count), 0)
    cols = lax.broadcasted_iota(jnp.int32, (count, count), 1)
    row_rank = jnp.zeros((count, count), jnp.int32)
    col_rank = jnp.zeros((count, count), jnp.int32)
    same = jnp.zeros((count, count), jnp.int32)
    for k in range(m):
        in_row = (rows >= k * BW) & (rows < (k + 1) * BW)
        in_col = (cols >= k * BW) & (cols < (k + 1) * BW)
        row_rank = jnp.where(in_row, rank_ref[k], row_rank)
        col_rank = jnp.where(in_col, rank_ref[k], col_rank)
        same = jnp.where(in_row & in_col, 1, same)
    inside = (same == 1) & (cols < rows)
    return jnp.where((col_rank < row_rank) | inside, 1.0, 0.0).astype(F32)


def fused(
    n, m, rank_ref, act_ref, dir_ref, out_ref,
    feat, low, v32, u32, chain, part, arrived, proj, wsum, half, coef, sq_out, sq_in,
    f_loc, f_s, f_r, g_s, g_r, z_s, z_r, v_s, v_r, p_s, p_r, k_s, k_r, q_s, q_r,
):
    i, b = lax.axis_index("tok"), lax.axis_index("blk")
    tokens, rows = feat.shape[1], feat.shape[2]
    count = m * BW
    total_tokens, width = n * tokens, n * rows
    own = pl.ds(pl.multiple_of(b * BW, BW), BW)

    chips = n // 2

    def ahead(d):
        return lax.rem(i // 2 + d // 2, chips) * 2 + lax.rem(i + d, 2)

    def behind(d):
        return lax.rem(i // 2 + chips - d // 2, chips) * 2 + lax.rem(i + d, 2)

    def blk_ahead(d):
        return lax.rem(b + d, m)

    def blk_behind(d):
        return lax.rem(b + m - d, m)

    others = [(d, e) for e in range(m) for d in range(n) if (d, e) != (0, 0)]

    barrier = pltpu.get_barrier_semaphore()
    for d, e in others:
        pl.semaphore_signal(
            barrier, inc=1, device_id={"tok": ahead(d), "blk": blk_ahead(e)}, device_id_type=MESH
        )
    pl.semaphore_wait(barrier, len(others))

    sent = []

    def push(src, dst, s, r, d, e):
        copy = pltpu.make_async_remote_copy(
            src_ref=src, dst_ref=dst, send_sem=s[0].at[s[1:]], recv_sem=r[0].at[r[1:]],
            device_id={"tok": ahead(d), "blk": blk_ahead(e)}, device_id_type=MESH,
        )
        copy.start()
        sent.append(copy)

    def landed(dst, s, r):
        pltpu.make_async_remote_copy(
            src_ref=dst, dst_ref=dst, send_sem=s[0].at[s[1:]], recv_sem=r[0].at[r[1:]],
            device_id={"tok": ahead(1)}, device_id_type=MESH,
        ).wait_recv()

    direct = tokens // 2
    share = (tokens - direct) // m
    piece = pl.ds(pl.multiple_of(direct + b * share, share), share)

    def columns_of(d):
        return pl.ds(pl.multiple_of(ahead(d) * rows, 128), rows)

    for d in range(2, n):
        push(act_ref.at[piece, columns_of(d)], feat.at[i, piece], (g_s, d), (g_r, d), d, 0)
    for d in range(2, n):
        cols, top = columns_of(d), pl.ds(0, direct)
        push(act_ref.at[top, cols], feat.at[i, top], (f_s, d), (f_r, d), d, 0)
    push(act_ref.at[:, columns_of(1)], feat.at[i], (f_s, 1), (f_r, 1), 1, 0)
    mine = pltpu.make_async_copy(
        act_ref.at[:, pl.ds(pl.multiple_of(i * rows, 128), rows)], feat.at[i], f_loc
    )
    mine.start()
    v32[...] = dir_ref[...]
    low[own, :] = v32[...].astype(BF16)
    for d in range(2, n):
        here = feat.at[behind(d), piece]
        landed(here, (g_s, d), (g_r, d))
        for e in range(1, m):
            push(here, here, (z_s, d, e), (z_r, d, e), 0, e)
    for e in range(1, m):
        push(low.at[own], low.at[own], (v_s, e), (v_r, e), 0, e)

    def block_landed(d):
        j = behind(d)
        if d == 1:
            landed(feat.at[j], (f_s, d), (f_r, d))
            return
        landed(feat.at[j, pl.ds(0, direct)], (f_s, d), (f_r, d))
        for e in range(1, m):
            other = pl.ds(pl.multiple_of(direct + blk_behind(e) * share, share), share)
            landed(feat.at[j, other], (z_s, d, e), (z_r, d, e))

    mask = order_mask(rank_ref, m, count)
    mine.wait()

    def scatter(k, left, first):
        kept = nt(left, feat[i])
        for d in range(1, n):
            back = ((chips - d // 2) % chips) * 2 + d % 2
            j = ahead(d)
            if first:
                block_landed(back)
            part[k, d] = nt(left, feat[j])
            push(part.at[k, d], arrived.at[k, d], (p_s, k, d), (p_r, k, d), d, 0)
        return kept

    def gather(k, kept):
        for d in range(1, n):
            landed(arrived.at[k, d], (p_s, k, d), (p_r, k, d))
            kept = kept + arrived[k, d]
        chain[k, i, own, :] = kept.astype(BF16)
        tile = chain.at[k, i, own]
        for d in range(1, n):
            push(tile, tile, (k_s, k, d, 0), (k_r, k, d, 0), d, 0)
        for e in range(1, m):
            push(tile, tile, (k_s, k, 0, e), (k_r, k, 0, e), 0, e)

    def pass_on(k):
        for e in range(1, m):
            chain_landed(k, 0, e)
            peer = pl.ds(pl.multiple_of(blk_behind(e) * BW, BW), BW)
            tile = chain.at[k, i, peer]
            for d in range(1, n):
                push(tile, tile, (k_s, k, d, e), (k_r, k, d, e), d, 0)

    def chain_landed(k, d, e):
        peer = pl.ds(pl.multiple_of(blk_behind(e) * BW, BW), BW)
        landed(chain.at[k, behind(d), peer], (k_s, k, d, e), (k_r, k, d, e))

    def to_features(k):
        total = nn(chain[k, i, own, :], feat[i])
        for d in range(1, n):
            chain_landed(k, d, 0)
            j = behind(d)
            total = total + nn(chain[k, j, own, :], feat[j])
        return total * (0.5 / total_tokens)

    def rest_landed(k):
        for e in range(1, m):
            for d in range(1, n):
                chain_landed(k, d, e)

    def penalised(t, cross):
        half[t] = mask * cross * (0.5 / (total_tokens * width))

    def send_squares(t, moved, everyone):
        column = jnp.sum(moved * moved, axis=1, keepdims=True)
        block = jnp.concatenate(
            [jnp.broadcast_to(column, (BW, 128)), jnp.zeros((128 - BW, 128), F32)], axis=0
        )
        sq_in[t, 0, 0] = block.T[0:8]
        for d, e in others:
            if everyone or e == 0:
                push(sq_in.at[t, 0, 0], sq_in.at[t, d, e], (q_s, t, d, e), (q_r, t, d, e), d, e)

    def scale_of(t, e):
        total = sq_in[t, 0, e]
        for d in range(1, n):
            total = total + sq_in[t, d, e]
        column = jnp.broadcast_to(total[0:1], (128, 128)).T[0:BW]
        return lax.rsqrt(column * (1.0 / width) + 1e-06)

    def scales(t):
        for d, e in others:
            landed(sq_in.at[t, d, e], (q_s, t, d, e), (q_r, t, d, e))
        for e in range(m):
            where = pl.ds(pl.multiple_of(blk_behind(e) * BW, BW), BW)
            sq_out[where, :] = scale_of(t, e)
        return sq_out[:, 0:1]

    def combine(c_rows, weights):
        lane = lax.broadcasted_iota(jnp.int32, (BW, count), 1)
        line = lax.broadcasted_iota(jnp.int32, (BW, count), 0) + b * BW
        diag = jnp.sum(jnp.where(lane == line, c_rows, 0.0), axis=1, keepdims=True)
        off = jnp.where(lane == line, 0.0, c_rows)
        moved = diag * v32[...] + nn(off.astype(BF16), low[...])
        for j in range(n):
            moved = moved + nn(weights(j).astype(BF16), feat[j])
        return moved

    kept = scatter(0, low[own, :], True)
    gather(0, kept)
    u32[...] = to_features(0)
    kept = scatter(1, u32[...].astype(BF16), False)
    pass_on(0)
    gather(1, kept)
    second = to_features(1).astype(BF16)
    kept = scatter(2, second, False)
    pass_on(1)

    rest_landed(0)
    for e in range(1, m):
        peer = pl.ds(pl.multiple_of(blk_behind(e) * BW, BW), BW)
        landed(low.at[peer], (v_s, e), (v_r, e))
    cross = jnp.zeros((count, count), F32)
    for j in range(n):
        cross = cross + nt(chain[0, j], chain[0, j])
    penalised(0, cross)
    moved = v32[...] + u32[...] - nn(half[0, own, :].astype(BF16), low[...])
    send_squares(0, moved, True)
    gather(2, kept)
    pass_on(2)

    rest_landed(1)
    d0 = scales(0)
    h0 = half[0].astype(BF16)
    cross = jnp.zeros((count, count), F32)
    for j in range(n):
        k0 = chain[0, j]
        p1 = d0 * (k0.astype(F32) - nn(h0, k0) + chain[1, j].astype(F32))
        proj[j] = p1
        cross = cross + nt(p1.astype(BF16), p1.astype(BF16))
    penalised(1, cross)
    h1 = half[1].astype(BF16)
    eye = jnp.where(
        lax.broadcasted_iota(jnp.int32, (count, count), 0)
        == lax.broadcasted_iota(jnp.int32, (count, count), 1), 1.0, 0.0,
    )
    c1 = d0 * (eye - half[0])
    coef[...] = c1 - nn(h1, c1.astype(BF16))
    for j in range(n):
        w1 = d0 * chain[0, j].astype(F32) * (0.5 / total_tokens)
        wsum[j] = w1 - nn(h1, w1.astype(BF16)) + proj[j] * (0.5 / total_tokens)
    moved = combine(coef[own, :], lambda j: wsum[j, own, :])
    send_squares(1, moved, True)

    for d in range(1, n):
        chain_landed(2, d, 0)
    rest_landed(2)
    for j in range(n):
        k1 = chain[1, j]
        q1 = d0 * (k1.astype(F32) - nn(h0, k1) + chain[2, j].astype(F32))
        p1 = proj[j]
        proj[j] = p1 - nn(h1, p1.astype(BF16)) + q1
    d1 = scales(1)
    cross = jnp.zeros((count, count), F32)
    for j in range(n):
        p2 = d1 * proj[j]
        proj[j] = p2
        wsum[j] = d1 * wsum[j]
        cross = cross + nt(p2.astype(BF16), p2.astype(BF16))
    penalised(2, cross)
    coef[...] = d1 * coef[...]
    h2 = half[2, own, :].astype(BF16)
    c3 = coef[own, :] - nn(h2, coef[...].astype(BF16))

    def last_weights(j):
        return (
            wsum[j, own, :] - nn(h2, wsum[j].astype(BF16)) + proj[j, own, :] * (0.5 / total_tokens)
        )

    moved = combine(c3, last_weights)
    send_squares(2, moved, False)
    v32[...] = moved
    for d in range(1, n):
        landed(sq_in.at[2, d, 0], (q_s, 2, d, 0), (q_r, 2, d, 0))
    out_ref[...] = v32[...] * scale_of(2, 0)[:, 0:1]
    for copy in sent:
        copy.wait_send()


def fused_body(n, m, activations, directions, block_rank):
    tokens = activations.shape[0]
    rows = directions.shape[0]
    count = m * BW
    dma = pltpu.SemaphoreType.DMA
    return pl.pallas_call(
        functools.partial(fused, n, m),
        out_shape=jax.ShapeDtypeStruct((BW, rows), F32),
        in_specs=[
            pl.BlockSpec(memory_space=pltpu.SMEM),
            pl.BlockSpec(memory_space=pl.ANY),
            pl.BlockSpec(memory_space=pltpu.VMEM),
        ],
        out_specs=pl.BlockSpec(memory_space=pltpu.VMEM),
        scratch_shapes=[
            pltpu.VMEM((n, tokens, rows), BF16),
            pltpu.VMEM((count, rows), BF16),
            pltpu.VMEM((BW, rows), F32),
            pltpu.VMEM((BW, rows), F32),
            pltpu.VMEM((ITERS, n, count, tokens), BF16),
            pltpu.VMEM((ITERS, n, BW, tokens), F32),
            pltpu.VMEM((ITERS, n, BW, tokens), F32),
            pltpu.VMEM((n, count, tokens), F32),
            pltpu.VMEM((n, count, tokens), F32),
            pltpu.VMEM((ITERS, count, count), F32),
            pltpu.VMEM((count, count), F32),
            pltpu.VMEM((count, 128), F32),
            pltpu.VMEM((ITERS, n, m, 8, 128), F32),
            dma,
            dma((n,)), dma((n,)),
            dma((n,)), dma((n,)),
            dma((n, m)), dma((n, m)),
            dma((m,)), dma((m,)),
            dma((ITERS, n)), dma((ITERS, n)),
            dma((ITERS, n, m)), dma((ITERS, n, m)),
            dma((ITERS, n, m)), dma((ITERS, n, m)),
        ],
        compiler_params=pltpu.CompilerParams(
            collective_id=0, has_side_effects=True, vmem_limit_bytes=58 * 1024 * 1024
        ),
    )(block_rank, activations, directions.T).T


def solution(mesh):
    n, m = mesh.shape["tok"], mesh.shape["blk"]
    placed = (P(("groups", "tok"), None), P(("groups", "tok"), "blk"), P())

    def chosen(activations, directions, block_rank):
        held = n * m * BW * activations.shape[0] * (3 * 2 + 2 * 4)
        if held <= 16 * 1024 * 1024:
            return fused_body(n, m, activations, directions, block_rank)
        return body(activations, directions, block_rank)

    return jax.shard_map(
        chosen, mesh=mesh, in_specs=placed, out_specs=P(("groups", "tok"), "blk"), check_vma=False
    )
```

```python
import functools

import jax
import jax.numpy as jnp
from jax import lax
from jax.experimental import pallas as pl
from jax.experimental.pallas import tpu as pltpu
from jax.sharding import PartitionSpec as P

BW = 64
ITERS = 3


def block_ranks(block_rank, index):
    blocks = index // BW
    table = (blocks[:, None] == jnp.arange(block_rank.shape[0], dtype=jnp.int32)[None, :]).astype(
        jnp.int32
    )
    return (blocks, jnp.sum(table * block_rank[None, :], axis=1))


def split_parts(weighted):
    high = lax.optimization_barrier(weighted.astype(jnp.bfloat16))
    rest = (weighted - high.astype(jnp.float32)).astype(jnp.bfloat16)
    return (high, rest)


def body(activations, directions, block_rank):
    width = activations.shape[1]
    total_tokens = activations.shape[0] * lax.axis_size("tok")
    count = BW * lax.axis_size("blk")
    mine = lax.axis_index("blk")
    own_index = mine * BW + jnp.arange(BW, dtype=jnp.int32)
    all_index = jnp.arange(count, dtype=jnp.int32)
    own_blocks, own_ranks = block_ranks(block_rank, own_index)
    all_blocks, all_ranks = block_ranks(block_rank, all_index)
    contract = (((1,), (1,)), ((), ()))
    features = lax.all_to_all(activations, "tok", split_axis=1, concat_axis=0, tiled=True)
    current = directions
    for step in range(ITERS):
        low = current.astype(jnp.bfloat16)
        proj = jnp.dot(
            activations,
            lax.all_gather(low, "tok", axis=0, tiled=True),
            preferred_element_type=jnp.float32,
        ).astype(jnp.bfloat16)
        cov_dir = (
            lax.dot_general(
                features,
                lax.all_gather(proj, "tok", axis=0, tiled=True),
                (((0,), (0,)), ((), ())),
                preferred_element_type=jnp.float32,
            )
            / total_tokens
        )
        partial_rows = lax.dot_general(
            proj,
            lax.all_gather(proj, "blk", axis=1, tiled=True),
            (((0,), (0,)), ((), ())),
            preferred_element_type=jnp.float32,
        )
        cross_row = lax.psum(partial_rows, "tok") / (total_tokens * width)
        before = all_ranks[None, :] < own_ranks[:, None]
        inside = (all_blocks[None, :] == own_blocks[:, None]) & (
            all_index[None, :] < own_index[:, None]
        )
        high, rest = split_parts((before | inside).astype(jnp.float32) * cross_row)
        piece = lax.all_gather(low, "blk", axis=1, tiled=True)
        total = lax.dot_general(piece, high, contract, preferred_element_type=jnp.float32)
        penalty = total + lax.dot_general(piece, rest, contract, preferred_element_type=jnp.float32)
        moved = current + 0.5 * (cov_dir - penalty)
        squares = lax.psum(jnp.sum(moved * moved, axis=0), "tok")
        scale = jnp.sqrt(squares / width + 1e-06)
        current = moved / scale[None, :]
    return current


F32, BF16 = jnp.float32, jnp.bfloat16
MESH = pl.DeviceIdType.MESH


def nt(a, b):
    return lax.dot_general(a, b, (((1,), (1,)), ((), ())), preferred_element_type=F32)


def nn(a, b):
    return jnp.dot(a, b, preferred_element_type=F32)


def order_mask(rank_ref, m, count):
    rows = lax.broadcasted_iota(jnp.int32, (count, count), 0)
    cols = lax.broadcasted_iota(jnp.int32, (count, count), 1)
    row_rank = jnp.zeros((count, count), jnp.int32)
    col_rank = jnp.zeros((count, count), jnp.int32)
    same = jnp.zeros((count, count), jnp.int32)
    for k in range(m):
        in_row = (rows >= k * BW) & (rows < (k + 1) * BW)
        in_col = (cols >= k * BW) & (cols < (k + 1) * BW)
        row_rank = jnp.where(in_row, rank_ref[k], row_rank)
        col_rank = jnp.where(in_col, rank_ref[k], col_rank)
        same = jnp.where(in_row & in_col, 1, same)
    inside = (same == 1) & (cols < rows)
    return jnp.where((col_rank < row_rank) | inside, 1.0, 0.0).astype(F32)


def fused(
    n, m, rank_ref, act_ref, dir_ref, out_ref,
    feat, low, v32, u32, chain, part, arrived, proj, wsum, half, coef, sq_out, sq_in,
    f_loc, f_s, f_r, g_s, g_r, z_s, z_r, v_s, v_r, p_s, p_r, k_s, k_r, q_s, q_r,
):
    i, b = lax.axis_index("tok"), lax.axis_index("blk")
    tokens, rows = feat.shape[1], feat.shape[2]
    count = m * BW
    total_tokens, width = n * tokens, n * rows
    own = pl.ds(pl.multiple_of(b * BW, BW), BW)

    chips = n // 2

    def ahead(d):
        return lax.rem(i // 2 + d // 2, chips) * 2 + lax.rem(i + d, 2)

    def behind(d):
        return lax.rem(i // 2 + chips - d // 2, chips) * 2 + lax.rem(i + d, 2)

    def blk_ahead(d):
        return lax.rem(b + d, m)

    def blk_behind(d):
        return lax.rem(b + m - d, m)

    others = [(d, e) for e in range(m) for d in range(n) if (d, e) != (0, 0)]

    barrier = pltpu.get_barrier_semaphore()
    for d, e in others:
        pl.semaphore_signal(
            barrier, inc=1, device_id={"tok": ahead(d), "blk": blk_ahead(e)}, device_id_type=MESH
        )
    pl.semaphore_wait(barrier, len(others))

    sent = []

    def push(src, dst, s, r, d, e):
        copy = pltpu.make_async_remote_copy(
            src_ref=src, dst_ref=dst, send_sem=s[0].at[s[1:]], recv_sem=r[0].at[r[1:]],
            device_id={"tok": ahead(d), "blk": blk_ahead(e)}, device_id_type=MESH,
        )
        copy.start()
        sent.append(copy)

    def landed(dst, s, r):
        pltpu.make_async_remote_copy(
            src_ref=dst, dst_ref=dst, send_sem=s[0].at[s[1:]], recv_sem=r[0].at[r[1:]],
            device_id={"tok": ahead(1)}, device_id_type=MESH,
        ).wait_recv()

    direct = tokens * 3 // 4
    share = (tokens - direct) // m
    piece = pl.ds(pl.multiple_of(direct + b * share, share), share)

    def columns_of(d):
        return pl.ds(pl.multiple_of(ahead(d) * rows, 128), rows)

    for d in range(2, n):
        push(act_ref.at[piece, columns_of(d)], feat.at[i, piece], (g_s, d), (g_r, d), d, 0)
    for d in range(2, n):
        cols, top = columns_of(d), pl.ds(0, direct)
        push(act_ref.at[top, cols], feat.at[i, top], (f_s, d), (f_r, d), d, 0)
    push(act_ref.at[:, columns_of(1)], feat.at[i], (f_s, 1), (f_r, 1), 1, 0)
    mine = pltpu.make_async_copy(
        act_ref.at[:, pl.ds(pl.multiple_of(i * rows, 128), rows)], feat.at[i], f_loc
    )
    mine.start()
    v32[...] = dir_ref[...]
    low[own, :] = v32[...].astype(BF16)
    for e in range(1, m):
        push(low.at[own], low.at[own], (v_s, e), (v_r, e), 0, e)
    for d in range(2, n):
        here = feat.at[behind(d), piece]
        landed(here, (g_s, d), (g_r, d))
        for e in range(1, m):
            push(here, here, (z_s, d, e), (z_r, d, e), 0, e)

    def block_landed(d):
        j = behind(d)
        if d == 1:
            landed(feat.at[j], (f_s, d), (f_r, d))
            return
        landed(feat.at[j, pl.ds(0, direct)], (f_s, d), (f_r, d))
        for e in range(1, m):
            other = pl.ds(pl.multiple_of(direct + blk_behind(e) * share, share), share)
            landed(feat.at[j, other], (z_s, d, e), (z_r, d, e))

    mask = order_mask(rank_ref, m, count)
    mine.wait()

    def scatter(k, left, first):
        kept = nt(left, feat[i])
        for d in range(1, n):
            back = ((chips - d // 2) % chips) * 2 + d % 2
            j = ahead(d)
            if first:
                block_landed(back)
            part[k, d] = nt(left, feat[j])
            push(part.at[k, d], arrived.at[k, d], (p_s, k, d), (p_r, k, d), d, 0)
        return kept

    def gather(k, kept):
        for d in range(1, n):
            landed(arrived.at[k, d], (p_s, k, d), (p_r, k, d))
            kept = kept + arrived[k, d]
        chain[k, i, own, :] = kept.astype(BF16)
        tile = chain.at[k, i, own]
        for d in range(1, n):
            push(tile, tile, (k_s, k, d, 0), (k_r, k, d, 0), d, 0)
        for e in range(1, m):
            push(tile, tile, (k_s, k, 0, e), (k_r, k, 0, e), 0, e)

    def pass_on(k):
        for e in range(1, m):
            chain_landed(k, 0, e)
            peer = pl.ds(pl.multiple_of(blk_behind(e) * BW, BW), BW)
            tile = chain.at[k, i, peer]
            for d in range(1, n):
                push(tile, tile, (k_s, k, d, e), (k_r, k, d, e), d, 0)

    def chain_landed(k, d, e):
        peer = pl.ds(pl.multiple_of(blk_behind(e) * BW, BW), BW)
        landed(chain.at[k, behind(d), peer], (k_s, k, d, e), (k_r, k, d, e))

    def to_features(k):
        total = nn(chain[k, i, own, :], feat[i])
        for d in range(1, n):
            chain_landed(k, d, 0)
            j = behind(d)
            total = total + nn(chain[k, j, own, :], feat[j])
        return total * (0.5 / total_tokens)

    def rest_landed(k):
        for e in range(1, m):
            for d in range(1, n):
                chain_landed(k, d, e)

    def penalised(t, cross):
        half[t] = mask * cross * (0.5 / (total_tokens * width))

    def send_squares(t, moved, everyone):
        column = jnp.sum(moved * moved, axis=1, keepdims=True)
        block = jnp.concatenate(
            [jnp.broadcast_to(column, (BW, 128)), jnp.zeros((128 - BW, 128), F32)], axis=0
        )
        sq_in[t, 0, 0] = block.T[0:8]
        for d, e in others:
            if everyone or e == 0:
                push(sq_in.at[t, 0, 0], sq_in.at[t, d, e], (q_s, t, d, e), (q_r, t, d, e), d, e)

    def scale_of(t, e):
        total = sq_in[t, 0, e]
        for d in range(1, n):
            total = total + sq_in[t, d, e]
        column = jnp.broadcast_to(total[0:1], (128, 128)).T[0:BW]
        return lax.rsqrt(column * (1.0 / width) + 1e-06)

    def scales(t):
        for d, e in others:
            landed(sq_in.at[t, d, e], (q_s, t, d, e), (q_r, t, d, e))
        for e in range(m):
            where = pl.ds(pl.multiple_of(blk_behind(e) * BW, BW), BW)
            sq_out[where, :] = scale_of(t, e)
        return sq_out[:, 0:1]

    def combine(c_rows, weights):
        lane = lax.broadcasted_iota(jnp.int32, (BW, count), 1)
        line = lax.broadcasted_iota(jnp.int32, (BW, count), 0) + b * BW
        diag = jnp.sum(jnp.where(lane == line, c_rows, 0.0), axis=1, keepdims=True)
        off = jnp.where(lane == line, 0.0, c_rows)
        moved = diag * v32[...] + nn(off.astype(BF16), low[...])
        for j in range(n):
            moved = moved + nn(weights(j).astype(BF16), feat[j])
        return moved

    kept = scatter(0, low[own, :], True)
    gather(0, kept)
    u32[...] = to_features(0)
    kept = scatter(1, u32[...].astype(BF16), False)
    gather(1, kept)
    second = to_features(1).astype(BF16)
    kept = scatter(2, second, False)
    pass_on(0)
    gather(2, kept)
    pass_on(1)

    rest_landed(0)
    for e in range(1, m):
        peer = pl.ds(pl.multiple_of(blk_behind(e) * BW, BW), BW)
        landed(low.at[peer], (v_s, e), (v_r, e))
    cross = jnp.zeros((count, count), F32)
    for j in range(n):
        cross = cross + nt(chain[0, j], chain[0, j])
    penalised(0, cross)
    moved = v32[...] + u32[...] - nn(half[0, own, :].astype(BF16), low[...])
    send_squares(0, moved, True)
    pass_on(2)

    rest_landed(1)
    d0 = scales(0)
    h0 = half[0].astype(BF16)
    cross = jnp.zeros((count, count), F32)
    for j in range(n):
        k0 = chain[0, j]
        p1 = d0 * (k0.astype(F32) - nn(h0, k0) + chain[1, j].astype(F32))
        proj[j] = p1
        cross = cross + nt(p1.astype(BF16), p1.astype(BF16))
    penalised(1, cross)
    h1 = half[1].astype(BF16)
    eye = jnp.where(
        lax.broadcasted_iota(jnp.int32, (count, count), 0)
        == lax.broadcasted_iota(jnp.int32, (count, count), 1), 1.0, 0.0,
    )
    c1 = d0 * (eye - half[0])
    coef[...] = c1 - nn(h1, c1.astype(BF16))
    for j in range(n):
        w1 = d0 * chain[0, j].astype(F32) * (0.5 / total_tokens)
        wsum[j] = w1 - nn(h1, w1.astype(BF16)) + proj[j] * (0.5 / total_tokens)
    moved = combine(coef[own, :], lambda j: wsum[j, own, :])
    send_squares(1, moved, True)

    for d in range(1, n):
        chain_landed(2, d, 0)
    rest_landed(2)
    for j in range(n):
        k1 = chain[1, j]
        q1 = d0 * (k1.astype(F32) - nn(h0, k1) + chain[2, j].astype(F32))
        p1 = proj[j]
        proj[j] = p1 - nn(h1, p1.astype(BF16)) + q1
    d1 = scales(1)
    cross = jnp.zeros((count, count), F32)
    for j in range(n):
        p2 = d1 * proj[j]
        proj[j] = p2
        wsum[j] = d1 * wsum[j]
        cross = cross + nt(p2.astype(BF16), p2.astype(BF16))
    penalised(2, cross)
    coef[...] = d1 * coef[...]
    h2 = half[2, own, :].astype(BF16)
    c3 = coef[own, :] - nn(h2, coef[...].astype(BF16))

    def last_weights(j):
        return (
            wsum[j, own, :] - nn(h2, wsum[j].astype(BF16)) + proj[j, own, :] * (0.5 / total_tokens)
        )

    moved = combine(c3, last_weights)
    send_squares(2, moved, False)
    v32[...] = moved
    for d in range(1, n):
        landed(sq_in.at[2, d, 0], (q_s, 2, d, 0), (q_r, 2, d, 0))
    out_ref[...] = v32[...] * scale_of(2, 0)[:, 0:1]
    for copy in sent:
        copy.wait_send()


def fused_body(n, m, activations, directions, block_rank):
    tokens = activations.shape[0]
    rows = directions.shape[0]
    count = m * BW
    dma = pltpu.SemaphoreType.DMA
    return pl.pallas_call(
        functools.partial(fused, n, m),
        out_shape=jax.ShapeDtypeStruct((BW, rows), F32),
        in_specs=[
            pl.BlockSpec(memory_space=pltpu.SMEM),
            pl.BlockSpec(memory_space=pl.ANY),
            pl.BlockSpec(memory_space=pltpu.VMEM),
        ],
        out_specs=pl.BlockSpec(memory_space=pltpu.VMEM),
        scratch_shapes=[
            pltpu.VMEM((n, tokens, rows), BF16),
            pltpu.VMEM((count, rows), BF16),
            pltpu.VMEM((BW, rows), F32),
            pltpu.VMEM((BW, rows), F32),
            pltpu.VMEM((ITERS, n, count, tokens), BF16),
            pltpu.VMEM((ITERS, n, BW, tokens), F32),
            pltpu.VMEM((ITERS, n, BW, tokens), F32),
            pltpu.VMEM((n, count, tokens), F32),
            pltpu.VMEM((n, count, tokens), F32),
            pltpu.VMEM((ITERS, count, count), F32),
            pltpu.VMEM((count, count), F32),
            pltpu.VMEM((count, 128), F32),
            pltpu.VMEM((ITERS, n, m, 8, 128), F32),
            dma,
            dma((n,)), dma((n,)),
            dma((n,)), dma((n,)),
            dma((n, m)), dma((n, m)),
            dma((m,)), dma((m,)),
            dma((ITERS, n)), dma((ITERS, n)),
            dma((ITERS, n, m)), dma((ITERS, n, m)),
            dma((ITERS, n, m)), dma((ITERS, n, m)),
        ],
        compiler_params=pltpu.CompilerParams(
            collective_id=0, has_side_effects=True, vmem_limit_bytes=58 * 1024 * 1024
        ),
    )(block_rank, activations, directions.T).T


def solution(mesh):
    n, m = mesh.shape["tok"], mesh.shape["blk"]
    placed = (P(("groups", "tok"), None), P(("groups", "tok"), "blk"), P())

    def chosen(activations, directions, block_rank):
        held = n * m * BW * activations.shape[0] * (3 * 2 + 2 * 4)
        if held <= 16 * 1024 * 1024 and activations.shape[0] % (64 * m) == 0:
            return fused_body(n, m, activations, directions, block_rank)
        return body(activations, directions, block_rank)

    return jax.shard_map(
        chosen, mesh=mesh, in_specs=placed, out_specs=P(("groups", "tok"), "blk"), check_vma=False
    )
```

```python
import functools

import jax
import jax.numpy as jnp
from jax import lax
from jax.experimental import pallas as pl
from jax.experimental.pallas import tpu as pltpu
from jax.sharding import PartitionSpec as P

BW = 64
ITERS = 3


def block_ranks(block_rank, index):
    blocks = index // BW
    table = (blocks[:, None] == jnp.arange(block_rank.shape[0], dtype=jnp.int32)[None, :]).astype(
        jnp.int32
    )
    return (blocks, jnp.sum(table * block_rank[None, :], axis=1))


def split_parts(weighted):
    high = lax.optimization_barrier(weighted.astype(jnp.bfloat16))
    rest = (weighted - high.astype(jnp.float32)).astype(jnp.bfloat16)
    return (high, rest)


def body(activations, directions, block_rank):
    width = activations.shape[1]
    total_tokens = activations.shape[0] * lax.axis_size("tok")
    count = BW * lax.axis_size("blk")
    mine = lax.axis_index("blk")
    own_index = mine * BW + jnp.arange(BW, dtype=jnp.int32)
    all_index = jnp.arange(count, dtype=jnp.int32)
    own_blocks, own_ranks = block_ranks(block_rank, own_index)
    all_blocks, all_ranks = block_ranks(block_rank, all_index)
    contract = (((1,), (1,)), ((), ()))
    features = lax.all_to_all(activations, "tok", split_axis=1, concat_axis=0, tiled=True)
    current = directions
    for step in range(ITERS):
        low = current.astype(jnp.bfloat16)
        proj = jnp.dot(
            activations,
            lax.all_gather(low, "tok", axis=0, tiled=True),
            preferred_element_type=jnp.float32,
        ).astype(jnp.bfloat16)
        cov_dir = (
            lax.dot_general(
                features,
                lax.all_gather(proj, "tok", axis=0, tiled=True),
                (((0,), (0,)), ((), ())),
                preferred_element_type=jnp.float32,
            )
            / total_tokens
        )
        partial_rows = lax.dot_general(
            proj,
            lax.all_gather(proj, "blk", axis=1, tiled=True),
            (((0,), (0,)), ((), ())),
            preferred_element_type=jnp.float32,
        )
        cross_row = lax.psum(partial_rows, "tok") / (total_tokens * width)
        before = all_ranks[None, :] < own_ranks[:, None]
        inside = (all_blocks[None, :] == own_blocks[:, None]) & (
            all_index[None, :] < own_index[:, None]
        )
        high, rest = split_parts((before | inside).astype(jnp.float32) * cross_row)
        piece = lax.all_gather(low, "blk", axis=1, tiled=True)
        total = lax.dot_general(piece, high, contract, preferred_element_type=jnp.float32)
        penalty = total + lax.dot_general(piece, rest, contract, preferred_element_type=jnp.float32)
        moved = current + 0.5 * (cov_dir - penalty)
        squares = lax.psum(jnp.sum(moved * moved, axis=0), "tok")
        scale = jnp.sqrt(squares / width + 1e-06)
        current = moved / scale[None, :]
    return current


F32, BF16 = jnp.float32, jnp.bfloat16
MESH = pl.DeviceIdType.MESH


def nt(a, b):
    return lax.dot_general(a, b, (((1,), (1,)), ((), ())), preferred_element_type=F32)


def nn(a, b):
    return jnp.dot(a, b, preferred_element_type=F32)


def order_mask(rank_ref, m, count):
    rows = lax.broadcasted_iota(jnp.int32, (count, count), 0)
    cols = lax.broadcasted_iota(jnp.int32, (count, count), 1)
    row_rank = jnp.zeros((count, count), jnp.int32)
    col_rank = jnp.zeros((count, count), jnp.int32)
    same = jnp.zeros((count, count), jnp.int32)
    for k in range(m):
        in_row = (rows >= k * BW) & (rows < (k + 1) * BW)
        in_col = (cols >= k * BW) & (cols < (k + 1) * BW)
        row_rank = jnp.where(in_row, rank_ref[k], row_rank)
        col_rank = jnp.where(in_col, rank_ref[k], col_rank)
        same = jnp.where(in_row & in_col, 1, same)
    inside = (same == 1) & (cols < rows)
    return jnp.where((col_rank < row_rank) | inside, 1.0, 0.0).astype(F32)


def fused(
    n, m, rank_ref, act_ref, dir_ref, out_ref,
    feat, low, v32, u32, chain, part, arrived, proj, wsum, half, coef, sq_out, sq_in,
    f_loc, f_s, f_r, g_s, g_r, z_s, z_r, v_s, v_r, p_s, p_r, k_s, k_r, q_s, q_r,
):
    i, b = lax.axis_index("tok"), lax.axis_index("blk")
    tokens, rows = feat.shape[1], feat.shape[2]
    count = m * BW
    total_tokens, width = n * tokens, n * rows
    own = pl.ds(pl.multiple_of(b * BW, BW), BW)

    chips = n // 2

    def ahead(d):
        return lax.rem(i // 2 + d // 2, chips) * 2 + lax.rem(i + d, 2)

    def behind(d):
        return lax.rem(i // 2 + chips - d // 2, chips) * 2 + lax.rem(i + d, 2)

    def blk_ahead(d):
        return lax.rem(b + d, m)

    def blk_behind(d):
        return lax.rem(b + m - d, m)

    others = [(d, e) for e in range(m) for d in range(n) if (d, e) != (0, 0)]

    barrier = pltpu.get_barrier_semaphore()
    for d, e in others:
        pl.semaphore_signal(
            barrier, inc=1, device_id={"tok": ahead(d), "blk": blk_ahead(e)}, device_id_type=MESH
        )
    pl.semaphore_wait(barrier, len(others))

    sent = []

    def push(src, dst, s, r, d, e):
        copy = pltpu.make_async_remote_copy(
            src_ref=src, dst_ref=dst, send_sem=s[0].at[s[1:]], recv_sem=r[0].at[r[1:]],
            device_id={"tok": ahead(d), "blk": blk_ahead(e)}, device_id_type=MESH,
        )
        copy.start()
        sent.append(copy)

    def landed(dst, s, r):
        pltpu.make_async_remote_copy(
            src_ref=dst, dst_ref=dst, send_sem=s[0].at[s[1:]], recv_sem=r[0].at[r[1:]],
            device_id={"tok": ahead(1)}, device_id_type=MESH,
        ).wait_recv()

    direct = tokens * 3 // 4
    share = (tokens - direct) // m
    piece = pl.ds(pl.multiple_of(direct + b * share, share), share)

    def columns_of(d):
        return pl.ds(pl.multiple_of(ahead(d) * rows, 128), rows)

    for d in range(2, n):
        push(act_ref.at[piece, columns_of(d)], feat.at[i, piece], (g_s, d), (g_r, d), d, 0)
    for d in range(2, n):
        cols, top = columns_of(d), pl.ds(0, direct)
        push(act_ref.at[top, cols], feat.at[i, top], (f_s, d), (f_r, d), d, 0)
    push(act_ref.at[:, columns_of(1)], feat.at[i], (f_s, 1), (f_r, 1), 1, 0)
    mine = pltpu.make_async_copy(
        act_ref.at[:, pl.ds(pl.multiple_of(i * rows, 128), rows)], feat.at[i], f_loc
    )
    mine.start()
    v32[...] = dir_ref[...]
    low[own, :] = v32[...].astype(BF16)
    for e in range(1, m):
        push(low.at[own], low.at[own], (v_s, e), (v_r, e), 0, e)
    for d in range(2, n):
        here = feat.at[behind(d), piece]
        landed(here, (g_s, d), (g_r, d))
        for e in range(1, m):
            push(here, here, (z_s, d, e), (z_r, d, e), 0, e)

    def block_landed(d):
        j = behind(d)
        if d == 1:
            landed(feat.at[j], (f_s, d), (f_r, d))
            return
        landed(feat.at[j, pl.ds(0, direct)], (f_s, d), (f_r, d))
        for e in range(1, m):
            other = pl.ds(pl.multiple_of(direct + blk_behind(e) * share, share), share)
            landed(feat.at[j, other], (z_s, d, e), (z_r, d, e))

    mask = order_mask(rank_ref, m, count)
    mine.wait()

    def scatter(k, left, first):
        kept = nt(left, feat[i])
        for d in range(1, n):
            back = ((chips - d // 2) % chips) * 2 + d % 2
            j = ahead(d)
            if first:
                block_landed(back)
            part[k, d] = nt(left, feat[j]).astype(BF16)
            push(part.at[k, d], arrived.at[k, d], (p_s, k, d), (p_r, k, d), d, 0)
        return kept

    def gather(k, kept):
        for d in range(1, n):
            landed(arrived.at[k, d], (p_s, k, d), (p_r, k, d))
            kept = kept + arrived[k, d].astype(F32)
        chain[k, i, own, :] = kept.astype(BF16)
        tile = chain.at[k, i, own]
        for d in range(1, n):
            push(tile, tile, (k_s, k, d, 0), (k_r, k, d, 0), d, 0)
        for e in range(1, m):
            push(tile, tile, (k_s, k, 0, e), (k_r, k, 0, e), 0, e)

    def pass_on(k):
        for e in range(1, m):
            chain_landed(k, 0, e)
            peer = pl.ds(pl.multiple_of(blk_behind(e) * BW, BW), BW)
            tile = chain.at[k, i, peer]
            for d in range(1, n):
                push(tile, tile, (k_s, k, d, e), (k_r, k, d, e), d, 0)

    def chain_landed(k, d, e):
        peer = pl.ds(pl.multiple_of(blk_behind(e) * BW, BW), BW)
        landed(chain.at[k, behind(d), peer], (k_s, k, d, e), (k_r, k, d, e))

    def to_features(k):
        total = nn(chain[k, i, own, :], feat[i])
        for d in range(1, n):
            chain_landed(k, d, 0)
            j = behind(d)
            total = total + nn(chain[k, j, own, :], feat[j])
        return total * (0.5 / total_tokens)

    def rest_landed(k):
        for e in range(1, m):
            for d in range(1, n):
                chain_landed(k, d, e)

    def penalised(t, cross):
        half[t] = mask * cross * (0.5 / (total_tokens * width))

    def send_squares(t, moved, everyone):
        column = jnp.sum(moved * moved, axis=1, keepdims=True)
        block = jnp.concatenate(
            [jnp.broadcast_to(column, (BW, 128)), jnp.zeros((128 - BW, 128), F32)], axis=0
        )
        sq_in[t, 0, 0] = block.T[0:8]
        for d, e in others:
            if everyone or e == 0:
                push(sq_in.at[t, 0, 0], sq_in.at[t, d, e], (q_s, t, d, e), (q_r, t, d, e), d, e)

    def scale_of(t, e):
        total = sq_in[t, 0, e]
        for d in range(1, n):
            total = total + sq_in[t, d, e]
        column = jnp.broadcast_to(total[0:1], (128, 128)).T[0:BW]
        return lax.rsqrt(column * (1.0 / width) + 1e-06)

    def scales(t):
        for d, e in others:
            landed(sq_in.at[t, d, e], (q_s, t, d, e), (q_r, t, d, e))
        for e in range(m):
            where = pl.ds(pl.multiple_of(blk_behind(e) * BW, BW), BW)
            sq_out[where, :] = scale_of(t, e)
        return sq_out[:, 0:1]

    def combine(c_rows, weights):
        lane = lax.broadcasted_iota(jnp.int32, (BW, count), 1)
        line = lax.broadcasted_iota(jnp.int32, (BW, count), 0) + b * BW
        diag = jnp.sum(jnp.where(lane == line, c_rows, 0.0), axis=1, keepdims=True)
        off = jnp.where(lane == line, 0.0, c_rows)
        moved = diag * v32[...] + nn(off.astype(BF16), low[...])
        for j in range(n):
            moved = moved + nn(weights(j).astype(BF16), feat[j])
        return moved

    kept = scatter(0, low[own, :], True)
    gather(0, kept)
    u32[...] = to_features(0)
    kept = scatter(1, u32[...].astype(BF16), False)
    gather(1, kept)
    second = to_features(1).astype(BF16)
    kept = scatter(2, second, False)
    pass_on(0)
    gather(2, kept)
    pass_on(1)

    rest_landed(0)
    for e in range(1, m):
        peer = pl.ds(pl.multiple_of(blk_behind(e) * BW, BW), BW)
        landed(low.at[peer], (v_s, e), (v_r, e))
    cross = jnp.zeros((count, count), F32)
    for j in range(n):
        cross = cross + nt(chain[0, j], chain[0, j])
    penalised(0, cross)
    moved = v32[...] + u32[...] - nn(half[0, own, :].astype(BF16), low[...])
    send_squares(0, moved, True)
    pass_on(2)

    rest_landed(1)
    d0 = scales(0)
    h0 = half[0].astype(BF16)
    cross = jnp.zeros((count, count), F32)
    for j in range(n):
        k0 = chain[0, j]
        p1 = d0 * (k0.astype(F32) - nn(h0, k0) + chain[1, j].astype(F32))
        proj[j] = p1
        cross = cross + nt(p1.astype(BF16), p1.astype(BF16))
    penalised(1, cross)
    h1 = half[1].astype(BF16)
    eye = jnp.where(
        lax.broadcasted_iota(jnp.int32, (count, count), 0)
        == lax.broadcasted_iota(jnp.int32, (count, count), 1), 1.0, 0.0,
    )
    c1 = d0 * (eye - half[0])
    coef[...] = c1 - nn(h1, c1.astype(BF16))
    for j in range(n):
        w1 = d0 * chain[0, j].astype(F32) * (0.5 / total_tokens)
        wsum[j] = w1 - nn(h1, w1.astype(BF16)) + proj[j] * (0.5 / total_tokens)
    moved = combine(coef[own, :], lambda j: wsum[j, own, :])
    send_squares(1, moved, True)

    for d in range(1, n):
        chain_landed(2, d, 0)
    rest_landed(2)
    for j in range(n):
        k1 = chain[1, j]
        q1 = d0 * (k1.astype(F32) - nn(h0, k1) + chain[2, j].astype(F32))
        p1 = proj[j]
        proj[j] = p1 - nn(h1, p1.astype(BF16)) + q1
    d1 = scales(1)
    cross = jnp.zeros((count, count), F32)
    for j in range(n):
        p2 = d1 * proj[j]
        proj[j] = p2
        wsum[j] = d1 * wsum[j]
        cross = cross + nt(p2.astype(BF16), p2.astype(BF16))
    penalised(2, cross)
    coef[...] = d1 * coef[...]
    h2 = half[2, own, :].astype(BF16)
    c3 = coef[own, :] - nn(h2, coef[...].astype(BF16))

    def last_weights(j):
        return (
            wsum[j, own, :] - nn(h2, wsum[j].astype(BF16)) + proj[j, own, :] * (0.5 / total_tokens)
        )

    moved = combine(c3, last_weights)
    send_squares(2, moved, False)
    v32[...] = moved
    for d in range(1, n):
        landed(sq_in.at[2, d, 0], (q_s, 2, d, 0), (q_r, 2, d, 0))
    out_ref[...] = v32[...] * scale_of(2, 0)[:, 0:1]
    for copy in sent:
        copy.wait_send()


def fused_body(n, m, activations, directions, block_rank):
    tokens = activations.shape[0]
    rows = directions.shape[0]
    count = m * BW
    dma = pltpu.SemaphoreType.DMA
    return pl.pallas_call(
        functools.partial(fused, n, m),
        out_shape=jax.ShapeDtypeStruct((BW, rows), F32),
        in_specs=[
            pl.BlockSpec(memory_space=pltpu.SMEM),
            pl.BlockSpec(memory_space=pl.ANY),
            pl.BlockSpec(memory_space=pltpu.VMEM),
        ],
        out_specs=pl.BlockSpec(memory_space=pltpu.VMEM),
        scratch_shapes=[
            pltpu.VMEM((n, tokens, rows), BF16),
            pltpu.VMEM((count, rows), BF16),
            pltpu.VMEM((BW, rows), F32),
            pltpu.VMEM((BW, rows), F32),
            pltpu.VMEM((ITERS, n, count, tokens), BF16),
            pltpu.VMEM((ITERS, n, BW, tokens), BF16),
            pltpu.VMEM((ITERS, n, BW, tokens), BF16),
            pltpu.VMEM((n, count, tokens), F32),
            pltpu.VMEM((n, count, tokens), F32),
            pltpu.VMEM((ITERS, count, count), F32),
            pltpu.VMEM((count, count), F32),
            pltpu.VMEM((count, 128), F32),
            pltpu.VMEM((ITERS, n, m, 8, 128), F32),
            dma,
            dma((n,)), dma((n,)),
            dma((n,)), dma((n,)),
            dma((n, m)), dma((n, m)),
            dma((m,)), dma((m,)),
            dma((ITERS, n)), dma((ITERS, n)),
            dma((ITERS, n, m)), dma((ITERS, n, m)),
            dma((ITERS, n, m)), dma((ITERS, n, m)),
        ],
        compiler_params=pltpu.CompilerParams(
            collective_id=0, has_side_effects=True, vmem_limit_bytes=58 * 1024 * 1024
        ),
    )(block_rank, activations, directions.T).T


def solution(mesh):
    n, m = mesh.shape["tok"], mesh.shape["blk"]
    placed = (P(("groups", "tok"), None), P(("groups", "tok"), "blk"), P())

    def chosen(activations, directions, block_rank):
        held = n * m * BW * activations.shape[0] * (3 * 2 + 2 * 4)
        if held <= 16 * 1024 * 1024 and activations.shape[0] % (64 * m) == 0:
            return fused_body(n, m, activations, directions, block_rank)
        return body(activations, directions, block_rank)

    return jax.shard_map(
        chosen, mesh=mesh, in_specs=placed, out_specs=P(("groups", "tok"), "blk"), check_vma=False
    )
```
